32 devices in a mesh: row: 4 (over y, core), col: 8 (over z, x).
Axes of the slice: x: 2, y: 2, z: 4, core: 2. Of those that a mesh axis runs over, the one named last changes fastest.
Arguments:
- rhs: bfloat16 [4, 4, 8, 64, 256], P(None, 'row', 'col'), may hold values from -6 to 6
- dinv: float32 [4, 4, 8, 64, 64], P(None, 'row', 'col'), may hold values from -1.5 to 1.5, as said below
- lower: bfloat16 [6, 4, 8, 8, 64, 128], P(None, 'row', 'col'), may hold values from -0.125 to 0.125
- sources: int32 [6, 4, 8, 8, 2], P(None, 'row', 'col'), may hold values from -1 to 3, as said below
Outputs:
- solution: float32 [4, 4, 8, 64, 256], P(None, 'row', 'col')
The draws below stay inside these ranges and needn't reach their ends.
Inputs may be any that keep to these rules, and one draw needn't show every extreme that they name: `dinv`: lower triangular. `sources`: for each level pair, holder and target, the live entries are distinct; in every level pair every device has a target with all 2 entries live.
All inputs are finite; a program needn't handle non-finite values.
Results may differ from the reference program's by a relative error of at most 0.002.
Values may be sent and summed in bfloat16 or wider, within the bound.
A program may use at most 64 MiB of HBM per device.

```python
import jax
import jax.numpy as jnp
from jax import lax

BS = 64
RHS = 256
LEVELS = 4
PER = 2
NR = 4
NC = 8
PAIRS = 6


def draw_dinv(key, part):
    key = jax.random.fold_in(key, 11)
    first, second = jax.random.split(key)
    shape = (LEVELS, NR, NC, BS, BS)
    below = jnp.arange(BS)[:, None] > jnp.arange(BS)[None, :]
    diagonal_mask = jnp.arange(BS)[:, None] == jnp.arange(BS)[None, :]
    spread = jnp.clip(jax.random.normal(first, shape, jnp.float32), -4.0, 4.0) * (0.5 / BS ** 0.5)
    diagonal = jax.random.uniform(second, shape[:-1], jnp.float32, 0.6, 1.4)
    return jnp.where(below, spread, 0.0) + jnp.where(diagonal_mask, diagonal[..., None], 0.0)


def draw_sources(key, part):
    key = jax.random.fold_in(key, 23)
    first, second, third = jax.random.split(key, 3)
    scores = jax.random.randint(first, (PAIRS, NR, NC, NC, NR), 0, 1 << 20) * NR + jnp.arange(NR, dtype=jnp.int32)
    ordering = jnp.argsort(scores, axis=-1)[..., :PER].astype(jnp.int32)
    counts = jax.random.randint(second, (PAIRS, NR, NC, NC), 0, PER + 1)
    filled = jax.random.randint(third, (PAIRS, NR, NC), 0, NC)
    counts = jnp.where(jnp.arange(NC) == filled[..., None], PER, counts)
    live = jnp.arange(PER) < counts[..., None]
    return jnp.where(live, ordering, -1).astype(jnp.int32)


def steps_of(own_key, dims, shards, least, top_value):
    def one(axis_at, blocks):
        heights = jax.random.uniform(jax.random.fold_in(jax.random.fold_in(own_key, 6), axis_at), (blocks,), jnp.float32, least / len(shards), top_value / len(shards))
        return jnp.repeat(jnp.exp(heights), dims[axis_at] // blocks).reshape((-1,) + (1,) * (len(dims) - axis_at - 1))

    level = one(*shards[0])
    for cut in shards[1:]:
        level = level * one(*cut)
    return level


def gaussian(rng, shape, width, most, pieces=(), kind=jnp.bfloat16):
    result = width * jax.random.normal(rng, shape, jnp.float32)
    if pieces:
        result = result * steps_of(rng, shape, pieces, -0.22, 0.18)
    return jnp.clip(result, -most, most).astype(kind)


def setup_inputs(seed: int = 0) -> dict:
    key_of = jax.random.split(jax.random.key(seed), 5)
    rhs = gaussian(key_of[0], (LEVELS, NR, NC, BS, RHS), 1.0, 6.0, ((1, 4), (2, 8)))
    dinv = draw_dinv(jax.random.fold_in(key_of[4], 71), 0)
    lower = gaussian(key_of[2], (PAIRS, NR, NC, NC, BS, PER * BS), (4 * BS * NC) ** -0.5, 0.125, ((1, 4), (2, 8)))
    sources = draw_sources(jax.random.fold_in(key_of[4], 71), 0)
    return {"rhs": rhs, "dinv": dinv, "lower": lower, "sources": sources}


def level_update(lower_pair, source_pair, solved):
    column_ids = jnp.arange(NC, dtype=jnp.int32)[:, None, None]

    def row_update(items):
        blocks, indices = items
        clipped = jnp.maximum(indices, 0).astype(jnp.int32)
        picked = solved[clipped, column_ids]
        picked = jnp.where((indices >= 0)[..., None, None], picked.astype(jnp.float32), jnp.float32(0.0))
        picked = picked.reshape(NC, NC, PER * BS, RHS)
        return jnp.einsum("cqik,cqkn->qin", blocks.astype(jnp.float32), picked)

    return lax.map(row_update, (lower_pair, source_pair))


def reference(rhs, dinv, lower, sources):
    accumulated = [jnp.zeros((NR, NC, BS, RHS), jnp.float32) for section in range(LEVELS)]
    results = []
    pair_index = 0
    for section in range(LEVELS):
        residual = rhs[section].astype(jnp.float32) - accumulated[section]
        solution = jnp.einsum("rcij,rcjn->rcin", dinv[section], residual, precision=lax.Precision.HIGHEST)
        results.append(solution)
        solved = solution.astype(jnp.bfloat16)
        for target in range(section + 1, LEVELS):
            accumulated[target] = accumulated[target] + level_update(lower[pair_index], sources[pair_index], solved)
            pair_index += 1
    return jnp.stack(results)
```

```python
import functools

import jax
import jax.numpy as jnp
from jax import lax
from jax.experimental import pallas as pl
from jax.experimental.pallas import tpu as pltpu
from jax.sharding import PartitionSpec as P

MESH = pl.DeviceIdType.MESH
BF16 = jnp.bfloat16
F32 = jnp.float32


def pair_of(levels, solved, target):
    return sum(levels - 1 - l for l in range(solved)) + target - solved - 1


def kernel(
    rows, groups, pair, parts,
    rhs, dinv, lower, sources, out,
    wide, held, gathered, outgoing, arrived, summed, far_sources, own_s, far_s,
    gsend, grecv, ssend, srecv, lsend, lrecv, csend, crecv, local_sem,
):
    levels, bs, width = rhs.shape
    part = width // parts
    last = levels - 1
    row = lax.axis_index("row")
    col = lax.axis_index("col")
    group = col // pair
    side = col % pair

    near = [(kr, kb) for kb in reversed(range(pair)) for kr in reversed(range(rows)) if (kr, kb) != (0, 0)]
    far = list(reversed(range(1, groups)))

    def near_device(kr, kb):
        return ((row + kr) % rows, group * pair + (side + kb) % pair)

    def far_device(ka):
        return (row, ((group + ka) % groups) * pair + side)

    barrier = pltpu.get_barrier_semaphore()
    for kr, kb in near:
        pl.semaphore_signal(barrier, inc=1, device_id=near_device(kr, kb), device_id_type=MESH)
    for ka in far:
        pl.semaphore_signal(barrier, inc=1, device_id=far_device(ka), device_id_type=MESH)

    def cols(h):
        return pl.ds(h * part, part)

    def solve(l, h):
        residual = rhs[l, :, cols(h)].astype(F32)
        if l > 0:
            acc = summed[h, group]
            for i in range(groups - 1):
                acc = acc + arrived[l - 1, h, i].astype(F32)
            residual = residual - acc
        solution = jnp.dot(
            dinv[l], residual, precision=lax.Precision.HIGHEST, preferred_element_type=F32
        )
        out[l, :, cols(h)] = solution
        if l < last:
            gathered[l, h, side, row] = solution.astype(BF16)

    def gather_copies(l, h):
        block = gathered.at[l, h, side, row]
        return [
            pltpu.make_async_remote_copy(
                src_ref=block, dst_ref=block,
                send_sem=gsend.at[l, h, i], recv_sem=grecv.at[l, h, i],
                device_id=near_device(kr, kb), device_id_type=MESH,
            )
            for i, (kr, kb) in enumerate(near)
        ]

    def scatter_copies(l, h):
        return [
            pltpu.make_async_remote_copy(
                src_ref=outgoing.at[l, h, (group + ka) % groups], dst_ref=arrived.at[l, h, i],
                send_sem=ssend.at[l, h, i], recv_sem=srecv.at[l, h, i],
                device_id=far_device(ka), device_id_type=MESH,
            )
            for i, ka in enumerate(far)
        ]

    def lower_copies(target):
        found = []
        for l in range(target):
            p = pair_of(levels, l, target)
            for kb in range(1, pair):
                found.append((p, pltpu.make_async_remote_copy(
                    src_ref=lower.at[p, :, (side + kb) % pair], dst_ref=held.at[p, kb - 1],
                    send_sem=lsend.at[p, kb - 1], recv_sem=lrecv.at[p, kb - 1],
                    device_id=near_device(0, kb), device_id_type=MESH,
                )))
        return found

    def source_copies():
        return [
            pltpu.make_async_remote_copy(
                src_ref=sources, dst_ref=far_sources.at[kb - 1],
                send_sem=csend.at[kb - 1], recv_sem=crecv.at[kb - 1],
                device_id=near_device(0, kb), device_id_type=MESH,
            )
            for kb in range(1, pair)
        ]

    lane = lax.broadcasted_iota(jnp.int32, (bs, 2 * bs), 1)
    first = lane < bs

    def spread(p, index_of, block_of, from_side):
        def one(g, carry):
            base = (g * pair + side) * 2
            s0 = index_of(base)
            s1 = index_of(base + 1)
            block = block_of(g)
            in_place = jnp.where(first, s0, s1)
            across = jnp.where(first, s1, s0)
            swapped = jnp.concatenate([block[:, bs:], block[:, :bs]], axis=1)
            for two in range(rows // 2):
                even, odd = 2 * two, 2 * two + 1
                wanted = jnp.where(first, even, odd)
                straight = jnp.where(in_place == wanted, 1.0, 0.0).astype(BF16)
                crossed = jnp.where(across == wanted, 1.0, 0.0).astype(BF16)
                wide[p, from_side, g, :, 2 * two * bs:(2 * two + 2) * bs] = (
                    block * straight + swapped * crossed
                )
            return carry

        if groups <= 4:
            for g in range(groups):
                one(g, 0)
        else:
            lax.fori_loop(0, groups, one, 0)

    def spread_own(target):
        for l in range(target):
            p = pair_of(levels, l, target)
            spread(p, lambda i, p=p: own_s[p, i], lambda g, p=p: lower[p, g, side], side)

    def spread_far(target):
        for p, copy in lower_copies(target):
            copy.wait_recv()
        for l in range(target):
            p = pair_of(levels, l, target)
            for kb in range(1, pair):
                spread(
                    p, lambda i, p=p, kb=kb: far_s[kb - 1, p, i],
                    lambda g, p=p, kb=kb: held[p, kb - 1, g],
                    (side + pair - kb) % pair,
                )

    chunk = min(groups, 4)

    def product(l, target, h, begin):
        p = pair_of(levels, l, target)
        total = None
        for s in range(pair):
            left = wide[p, s, pl.ds(begin, chunk)].reshape(chunk * bs, rows * bs)
            right = gathered[l, h, s].reshape(rows * bs, part)
            term = jnp.dot(left, right, preferred_element_type=F32)
            total = term if total is None else total + term
        return total.reshape(chunk, bs, part)

    def over_chunks(body):
        if groups == chunk:
            body(0)
        else:
            def step(i, carry):
                body(i * chunk)
                return carry
            lax.fori_loop(0, groups // chunk, step, 0)

    def earlier_terms(l, h):
        def body(begin):
            total = product(0, l + 1, h, begin)
            for m in range(1, l):
                total = total + product(m, l + 1, h, begin)
            summed[h, pl.ds(begin, chunk)] = total
        if l > 0:
            over_chunks(body)

    def newest_term(l, h):
        def body(begin):
            total = product(l, l + 1, h, begin)
            if l > 0:
                total = total + summed[h, pl.ds(begin, chunk)]
            summed[h, pl.ds(begin, chunk)] = total
            outgoing[l, h, pl.ds(begin, chunk)] = total.astype(BF16)
        over_chunks(body)

    own_copy = pltpu.make_async_copy(sources, own_s, local_sem.at[0])
    own_copy.start()
    for h in range(parts):
        solve(0, h)
    own_copy.wait()
    spread_own(1)
    pl.semaphore_wait(barrier, len(near) + len(far))
    for copy in source_copies():
        copy.start()

    for l in range(last):
        for h in range(parts):
            if l > 0:
                for copy in scatter_copies(l - 1, h):
                    copy.wait_recv()
                solve(l, h)
            for copy in gather_copies(l, h):
                copy.start()
            if l == 0 and h == 0:
                for p, copy in lower_copies(1):
                    copy.start()
        if l == 0:
            for i, copy in enumerate(source_copies()):
                copy.wait_recv()
                back = pltpu.make_async_copy(far_sources.at[i], far_s.at[i], local_sem.at[1 + i])
                back.start()
                back.wait()
        spread_far(l + 1)
        for h in range(parts):
            earlier_terms(l, h)
        for h in range(parts):
            for copy in gather_copies(l, h):
                copy.wait_recv()
            newest_term(l, h)
            for copy in scatter_copies(l, h):
                copy.start()
        if l + 1 < last:
            for p, copy in lower_copies(l + 2):
                copy.start()
            spread_own(l + 2)
    for h in range(parts):
        for copy in scatter_copies(last - 1, h):
            copy.wait_recv()
        solve(last, h)

    for copy in source_copies():
        copy.wait_send()
    for l in range(last):
        for p, copy in lower_copies(l + 1):
            copy.wait_send()
        for h in range(parts):
            for copy in gather_copies(l, h) + scatter_copies(l, h):
                copy.wait_send()


def on_device(rows, columns, rhs, dinv, lower, sources):
    levels, _, _, bs, width = rhs.shape
    pairs = lower.shape[0]
    per = sources.shape[-1]
    pair = 2
    parts = 2
    groups = columns // pair
    part = width // parts
    last = levels - 1
    near = rows * pair - 1
    far = groups - 1
    dma = pltpu.SemaphoreType.DMA
    flops = 2 * pairs * groups * bs * pair * rows * bs * width
    result = pl.pallas_call(
        functools.partial(kernel, rows, groups, pair, parts),
        out_shape=jax.ShapeDtypeStruct((levels, bs, width), F32),
        in_specs=[pl.BlockSpec(memory_space=pltpu.VMEM)] * 4,
        out_specs=pl.BlockSpec(memory_space=pltpu.VMEM),
        scratch_shapes=[
            pltpu.VMEM((pairs, pair, groups, bs, rows * bs), BF16),
            pltpu.VMEM((pairs, pair - 1, groups, bs, per * bs), BF16),
            pltpu.VMEM((last, parts, pair, rows, bs, part), BF16),
            pltpu.VMEM((last, parts, groups, bs, part), BF16),
            pltpu.VMEM((last, parts, far, bs, part), BF16),
            pltpu.VMEM((parts, groups, bs, part), F32),
            pltpu.VMEM((pair - 1, pairs, columns * per), jnp.int32),
            pltpu.SMEM((pairs, columns * per), jnp.int32),
            pltpu.SMEM((pair - 1, pairs, columns * per), jnp.int32),
            dma((last, parts, near)),
            dma((last, parts, near)),
            dma((last, parts, far)),
            dma((last, parts, far)),
            dma((pairs, pair - 1)),
            dma((pairs, pair - 1)),
            dma((pair - 1,)),
            dma((pair - 1,)),
            dma((pair,)),
        ],
        compiler_params=pltpu.CompilerParams(
            collective_id=0, has_side_effects=True, vmem_limit_bytes=48 * 1024 * 1024
        ),
        cost_estimate=pl.CostEstimate(
            flops=flops, bytes_accessed=2 * lower.size, transcendentals=0
        ),
    )(
        rhs.reshape(levels, bs, width),
        dinv.reshape(levels, bs, bs),
        lower.reshape(pairs, groups, pair, bs, per * bs),
        sources.reshape(pairs, columns * per),
    )
    return result.reshape(levels, 1, 1, bs, width)


def solution(mesh):
    in_specs = (
        P(None, "row", "col", None, None),
        P(None, "row", "col", None, None),
        P(None, "row", "col", None, None, None),
        P(None, "row", "col", None, None),
    )
    out_specs = P(None, "row", "col", None, None)
    return jax.shard_map(
        functools.partial(on_device, mesh.shape["row"], mesh.shape["col"]),
        mesh=mesh, in_specs=in_specs, out_specs=out_specs, check_vma=False,
    )
```

```python
import functools

import jax
import jax.numpy as jnp
from jax import lax
from jax.experimental import pallas as pl
from jax.experimental.pallas import tpu as pltpu
from jax.sharding import PartitionSpec as P

MESH = pl.DeviceIdType.MESH
BF16 = jnp.bfloat16
F32 = jnp.float32


def pair_of(levels, solved, target):
    return sum(levels - 1 - l for l in range(solved)) + target - solved - 1


def kernel(
    rows, groups, pair, parts,
    rhs_hbm, dinv_hbm, lower, sources, out_hbm,
    out, rhs, dinv, split, mine, wide, held, gathered, outgoing, arrived, summed,
    far_sources, own_s, far_s,
    gsend, grecv, ssend, srecv, lsend, lrecv, csend, crecv, local_sem, out_sem,
):
    levels, bs, width = rhs.shape
    part = width // parts
    last = levels - 1
    row = lax.axis_index("row")
    col = lax.axis_index("col")
    group = col // pair
    side = col % pair
    blocks = pair * rows

    loads = [
        pltpu.make_async_copy(rhs_hbm, rhs, local_sem.at[0]),
        pltpu.make_async_copy(dinv_hbm, dinv, local_sem.at[1]),
        pltpu.make_async_copy(sources, own_s, local_sem.at[2]),
        pltpu.make_async_copy(lower.at[0, :, side], mine.at[0], local_sem.at[3]),
        pltpu.make_async_copy(lower.at[1:, :, side], mine.at[1:], local_sem.at[4]),
    ]
    for load in loads:
        load.start()

    near = [(kr, kb) for kb in reversed(range(pair)) for kr in reversed(range(rows)) if (kr, kb) != (0, 0)]
    far = list(reversed(range(1, groups)))

    def near_device(kr, kb):
        return ((row + kr) % rows, group * pair + (side + kb) % pair)

    def far_device(ka):
        return (row, ((group + ka) % groups) * pair + side)

    barrier = pltpu.get_barrier_semaphore()
    for kr, kb in near:
        pl.semaphore_signal(barrier, inc=1, device_id=near_device(kr, kb), device_id_type=MESH)
    for ka in far:
        pl.semaphore_signal(barrier, inc=1, device_id=far_device(ka), device_id_type=MESH)

    def cols(h):
        return pl.ds(h * part, part)

    def result_copy(l, h):
        return pltpu.make_async_copy(
            out.at[l, :, cols(h)], out_hbm.at[l, :, cols(h)], out_sem.at[l, h]
        )

    def solve(l, h):
        residual = rhs[l, :, cols(h)].astype(F32)
        if l > 0:
            acc = summed[h, group]
            for i in range(groups - 1):
                acc = acc + arrived[l - 1, h, i].astype(F32)
            residual = residual - acc
        high = residual.astype(BF16)
        low = (residual - high.astype(F32)).astype(BF16)
        solution = jnp.dot(
            split[l], jnp.concatenate([high, low, high, low], axis=0),
            preferred_element_type=F32,
        )
        out[l, :, cols(h)] = solution
        if l < last:
            gathered[l, h, side * rows + row] = solution.astype(BF16)
        result_copy(l, h).start()

    def gather_copies(l, h):
        block = gathered.at[l, h, side * rows + row]
        return [
            pltpu.make_async_remote_copy(
                src_ref=block, dst_ref=block,
                send_sem=gsend.at[l], recv_sem=grecv.at[l, h],
                device_id=near_device(kr, kb), device_id_type=MESH,
            )
            for kr, kb in near
        ]

    def scatter_copies(l, h):
        return [
            pltpu.make_async_remote_copy(
                src_ref=outgoing.at[l, h, (group + ka) % groups], dst_ref=arrived.at[l, h, i],
                send_sem=ssend.at[l], recv_sem=srecv.at[l, h],
                device_id=far_device(ka), device_id_type=MESH,
            )
            for i, ka in enumerate(far)
        ]

    def bytes_of(ref, send_sem, recv_sem, device):
        return pltpu.make_async_remote_copy(
            src_ref=ref, dst_ref=ref, send_sem=send_sem, recv_sem=recv_sem,
            device_id=device, device_id_type=MESH,
        )

    def wait_gather(l, h):
        ref = gathered.at[l, h, pl.ds(0, blocks - 1)]
        bytes_of(ref, gsend.at[l], grecv.at[l, h], near_device(*near[0])).wait_recv()

    def wait_scatter(l, h):
        bytes_of(arrived.at[l, h], ssend.at[l], srecv.at[l, h], far_device(far[0])).wait_recv()

    def wait_sends(l):
        ref = gathered.at[l, :, pl.ds(0, blocks - 1)]
        bytes_of(ref, gsend.at[l], grecv.at[l, 0], near_device(*near[0])).wait_send()
        bytes_of(arrived.at[l], ssend.at[l], srecv.at[l, 0], far_device(far[0])).wait_send()

    def lower_copies(target):
        found = []
        for l in range(target):
            p = pair_of(levels, l, target)
            for kb in range(1, pair):
                found.append((p, pltpu.make_async_remote_copy(
                    src_ref=lower.at[p, :, (side + kb) % pair], dst_ref=held.at[p, kb - 1],
                    send_sem=lsend.at[p, kb - 1], recv_sem=lrecv.at[p, kb - 1],
                    device_id=near_device(0, kb), device_id_type=MESH,
                )))
        return found

    def source_copies():
        return [
            pltpu.make_async_remote_copy(
                src_ref=sources, dst_ref=far_sources.at[kb - 1],
                send_sem=csend.at[kb - 1], recv_sem=crecv.at[kb - 1],
                device_id=near_device(0, kb), device_id_type=MESH,
            )
            for kb in range(1, pair)
        ]

    lane = lax.broadcasted_iota(jnp.int32, (bs, 2 * bs), 1)
    first = lane < bs

    def spread(p, index_of, block_of, from_side):
        def one(g, carry):
            s0 = index_of(0, g * pair + side)
            s1 = index_of(1, g * pair + side)
            block = block_of(g)
            in_place = jnp.where(first, s0, s1)
            across = jnp.where(first, s1, s0)
            swapped = jnp.concatenate([block[:, bs:], block[:, :bs]], axis=1)
            for two in range(rows // 2):
                even, odd = 2 * two, 2 * two + 1
                wanted = jnp.where(first, even, odd)
                straight = jnp.where(in_place == wanted, 1.0, 0.0).astype(BF16)
                crossed = jnp.where(across == wanted, 1.0, 0.0).astype(BF16)
                wide[p, from_side, g, :, 2 * two * bs:(2 * two + 2) * bs] = (
                    block * straight + swapped * crossed
                )
            return carry

        if groups <= 4:
            for g in range(groups):
                one(g, 0)
        else:
            lax.fori_loop(0, groups, one, 0)

    def spread_own(target):
        for l in range(target):
            p = pair_of(levels, l, target)
            spread(p, lambda e, q, p=p: own_s[p, e, q], lambda g, p=p: mine[p, g], side)

    def spread_far(target):
        for p, copy in lower_copies(target):
            copy.wait_recv()
        for l in range(target):
            p = pair_of(levels, l, target)
            for kb in range(1, pair):
                spread(
                    p, lambda e, q, p=p, kb=kb: far_s[kb - 1, p, e, q],
                    lambda g, p=p, kb=kb: held[p, kb - 1, g],
                    (side + pair - kb) % pair,
                )

    chunk = min(groups, 4)

    def product(l, target, h, begin):
        p = pair_of(levels, l, target)
        total = None
        for s in range(pair):
            left = wide[p, s, pl.ds(begin, chunk)].reshape(chunk * bs, rows * bs)
            right = gathered[l, h, s * rows:(s + 1) * rows].reshape(rows * bs, part)
            term = jnp.dot(left, right, preferred_element_type=F32)
            total = term if total is None else total + term
        return total.reshape(chunk, bs, part)

    def over_chunks(body):
        if groups == chunk:
            body(0)
        else:
            def step(i, carry):
                body(i * chunk)
                return carry
            lax.fori_loop(0, groups // chunk, step, 0)

    def earlier_terms(l, h):
        def body(begin):
            total = product(0, l + 1, h, begin)
            for m in range(1, l):
                total = total + product(m, l + 1, h, begin)
            summed[h, pl.ds(begin, chunk)] = total
        if l > 0:
            over_chunks(body)

    def newest_term(l, h):
        def body(begin):
            total = product(l, l + 1, h, begin)
            if l > 0:
                total = total + summed[h, pl.ds(begin, chunk)]
            summed[h, pl.ds(begin, chunk)] = total
            outgoing[l, h, pl.ds(begin, chunk)] = total.astype(BF16)
        over_chunks(body)

    loads[0].wait()
    loads[1].wait()
    for l in range(levels):
        high = dinv[l].astype(BF16)
        low = (dinv[l] - high.astype(F32)).astype(BF16)
        split[l] = jnp.concatenate([high, high, low, low], axis=1)
    for h in range(parts):
        solve(0, h)
    loads[2].wait()
    loads[3].wait()
    spread_own(1)
    pl.semaphore_wait(barrier, len(near) + len(far))
    for copy in source_copies():
        copy.start()

    for l in range(last):
        for h in range(parts):
            if l > 0:
                wait_scatter(l - 1, h)
                solve(l, h)
            for copy in gather_copies(l, h):
                copy.start()
            if l == 0 and h == 0:
                for p, copy in lower_copies(1):
                    copy.start()
        if l == 0:
            for i, copy in enumerate(source_copies()):
                copy.wait_recv()
                back = pltpu.make_async_copy(far_sources.at[i], far_s.at[i], local_sem.at[5 + i])
                back.start()
                back.wait()
        spread_far(l + 1)
        for h in range(parts):
            earlier_terms(l, h)
        for h in range(parts):
            wait_gather(l, h)
            newest_term(l, h)
            for copy in scatter_copies(l, h):
                copy.start()
        if l + 1 < last:
            for p, copy in lower_copies(l + 2):
                copy.start()
            if l == 0:
                loads[4].wait()
            spread_own(l + 2)
            for p, copy in lower_copies(l + 1):
                copy.wait_send()
            if l > 0:
                wait_sends(l - 1)
    for copy in source_copies():
        copy.wait_send()
    for p, copy in lower_copies(last):
        copy.wait_send()
    for l in range(max(last - 2, 0), last - 1):
        wait_sends(l)
    for h in range(parts):
        wait_scatter(last - 1, h)
        solve(last, h)
    wait_sends(last - 1)
    for l in range(levels):
        for h in range(parts):
            result_copy(l, h).wait()


def on_device(rows, columns, rhs, dinv, lower, sources):
    levels, _, _, bs, width = rhs.shape
    pairs = lower.shape[0]
    per = sources.shape[-1]
    pair = 2
    parts = 2
    groups = columns // pair
    part = width // parts
    last = levels - 1
    far = groups - 1
    dma = pltpu.SemaphoreType.DMA
    flops = 2 * pairs * groups * bs * pair * rows * bs * width
    result = pl.pallas_call(
        functools.partial(kernel, rows, groups, pair, parts),
        out_shape=jax.ShapeDtypeStruct((levels, bs, width), F32),
        in_specs=[pl.BlockSpec(memory_space=pltpu.HBM)] * 4,
        out_specs=pl.BlockSpec(memory_space=pltpu.HBM),
        scratch_shapes=[
            pltpu.VMEM((levels, bs, width), F32),
            pltpu.VMEM((levels, bs, width), BF16),
            pltpu.VMEM((levels, bs, bs), F32),
            pltpu.VMEM((levels, bs, 4 * bs), BF16),
            pltpu.VMEM((pairs, groups, bs, per * bs), BF16),
            pltpu.VMEM((pairs, pair, groups, bs, rows * bs), BF16),
            pltpu.VMEM((pairs, pair - 1, groups, bs, per * bs), BF16),
            pltpu.VMEM((last, parts, pair * rows, bs, part), BF16),
            pltpu.VMEM((last, parts, groups, bs, part), BF16),
            pltpu.VMEM((last, parts, far, bs, part), BF16),
            pltpu.VMEM((parts, groups, bs, part), F32),
            pltpu.VMEM((pair - 1, pairs, per, columns), jnp.int32),
            pltpu.SMEM((pairs, per, columns), jnp.int32),
            pltpu.SMEM((pair - 1, pairs, per, columns), jnp.int32),
            dma((last,)),
            dma((last, parts)),
            dma((last,)),
            dma((last, parts)),
            dma((pairs, pair - 1)),
            dma((pairs, pair - 1)),
            dma((pair - 1,)),
            dma((pair - 1,)),
            dma((4 + pair,)),
            dma((levels, parts)),
        ],
        compiler_params=pltpu.CompilerParams(
            collective_id=0, has_side_effects=True, vmem_limit_bytes=64 * 1024 * 1024
        ),
        cost_estimate=pl.CostEstimate(
            flops=flops, bytes_accessed=2 * lower.size, transcendentals=0
        ),
    )(
        rhs.reshape(levels, bs, width),
        dinv.reshape(levels, bs, bs),
        lower.reshape(pairs, groups, pair, bs, per * bs),
        jnp.swapaxes(sources.reshape(pairs, columns, per), 1, 2),
    )
    return result.reshape(levels, 1, 1, bs, width)


def solution(mesh):
    in_specs = (
        P(None, "row", "col", None, None),
        P(None, "row", "col", None, None),
        P(None, "row", "col", None, None, None),
        P(None, "row", "col", None, None),
    )
    out_specs = P(None, "row", "col", None, None)
    return jax.shard_map(
        functools.partial(on_device, mesh.shape["row"], mesh.shape["col"]),
        mesh=mesh, in_specs=in_specs, out_specs=out_specs, check_vma=False,
    )
```

```python
import functools

import jax
import jax.numpy as jnp
from jax import lax
from jax.experimental import pallas as pl
from jax.experimental.pallas import tpu as pltpu
from jax.sharding import PartitionSpec as P

MESH = pl.DeviceIdType.MESH
BF16 = jnp.bfloat16
F32 = jnp.float32


def pair_of(levels, solved, target):
    return sum(levels - 1 - l for l in range(solved)) + target - solved - 1


def kernel(
    rows, groups, pair, parts,
    rhs_hbm, dinv_hbm, lower, sources, out,
    rhs, dinv, split, mine, wide, held, gathered, outgoing, arrived, summed,
    far_sources, own_s, far_s,
    gsend, grecv, ssend, srecv, lsend, lrecv, csend, crecv, local_sem, trecv,
):
    levels, bs, width = rhs.shape
    part = width // parts
    last = levels - 1
    row = lax.axis_index("row")
    col = lax.axis_index("col")
    group = col // pair
    side = col % pair
    blocks = pair * rows

    loads = [
        pltpu.make_async_copy(rhs_hbm, rhs, local_sem.at[0]),
        pltpu.make_async_copy(dinv_hbm, dinv, local_sem.at[1]),
        pltpu.make_async_copy(sources, own_s, local_sem.at[2]),
        pltpu.make_async_copy(lower.at[0, :, side], mine.at[0], local_sem.at[3]),
        pltpu.make_async_copy(lower.at[1:, :, side], mine.at[1:], local_sem.at[4]),
    ]
    for load in loads:
        load.start()

    near = [(kr, kb) for kb in reversed(range(pair)) for kr in reversed(range(0, rows, 2)) if (kr, kb) != (0, 0)]
    twin = (row + 1 - 2 * (row % 2), col)
    far = list(reversed(range(1, groups)))

    def near_device(kr, kb):
        return ((row + kr) % rows, group * pair + (side + kb) % pair)

    def far_device(ka):
        return (row, ((group + ka) % groups) * pair + side)

    barrier = pltpu.get_barrier_semaphore()
    for kr, kb in near:
        pl.semaphore_signal(barrier, inc=1, device_id=near_device(kr, kb), device_id_type=MESH)
    pl.semaphore_signal(barrier, inc=1, device_id=twin, device_id_type=MESH)
    for ka in far:
        pl.semaphore_signal(barrier, inc=1, device_id=far_device(ka), device_id_type=MESH)

    def cols(h):
        return pl.ds(h * part, part)

    def solve(l, h):
        residual = rhs[l, :, cols(h)].astype(F32)
        if l > 0:
            acc = summed[(l - 1) % 2, h, group]
            for i in range(groups - 1):
                acc = acc + arrived[l - 1, h, i].astype(F32)
            residual = residual - acc
        high = residual.astype(BF16)
        low = (residual - high.astype(F32)).astype(BF16)
        solution = jnp.dot(
            split[l], jnp.concatenate([high, low, high, low], axis=0),
            preferred_element_type=F32,
        )
        out[l, :, cols(h)] = solution
        if l < last:
            gathered[l, h, side * rows + row] = solution.astype(BF16)

    def gather_copies(l, h):
        block = gathered.at[l, h, side * rows + row]
        return [
            pltpu.make_async_remote_copy(
                src_ref=block, dst_ref=block,
                send_sem=gsend.at[l], recv_sem=grecv.at[l, h],
                device_id=near_device(kr, kb), device_id_type=MESH,
            )
            for kr, kb in near
        ] + [
            pltpu.make_async_remote_copy(
                src_ref=block, dst_ref=block,
                send_sem=gsend.at[l], recv_sem=trecv.at[l, h],
                device_id=twin, device_id_type=MESH,
            )
        ]

    def twin_copies(l, h):
        found = []
        for kr, kb in near:
            block = gathered.at[l, h, ((side + kb) % pair) * rows + (row + kr) % rows]
            found.append(pltpu.make_async_remote_copy(
                src_ref=block, dst_ref=block,
                send_sem=gsend.at[l], recv_sem=trecv.at[l, h],
                device_id=twin, device_id_type=MESH,
            ))
        return found

    def scatter_copies(l, h):
        return [
            pltpu.make_async_remote_copy(
                src_ref=outgoing.at[l, h, (group + ka) % groups], dst_ref=arrived.at[l, h, i],
                send_sem=ssend.at[l], recv_sem=srecv.at[l, h],
                device_id=far_device(ka), device_id_type=MESH,
            )
            for i, ka in enumerate(far)
        ]

    def bytes_of(ref, send_sem, recv_sem, device):
        return pltpu.make_async_remote_copy(
            src_ref=ref, dst_ref=ref, send_sem=send_sem, recv_sem=recv_sem,
            device_id=device, device_id_type=MESH,
        )

    def wait_gather(l, h):
        ref = gathered.at[l, h, pl.ds(0, len(near))]
        bytes_of(ref, gsend.at[l], grecv.at[l, h], near_device(*near[0])).wait_recv()

    def wait_twin(l, h):
        ref = gathered.at[l, h, pl.ds(0, len(near) + 1)]
        bytes_of(ref, gsend.at[l], trecv.at[l, h], twin).wait_recv()

    def wait_scatter(l, h):
        bytes_of(arrived.at[l, h], ssend.at[l], srecv.at[l, h], far_device(far[0])).wait_recv()

    def wait_sends(l):
        ref = gathered.at[l, :, pl.ds(0, blocks - 1)]
        bytes_of(ref, gsend.at[l], grecv.at[l, 0], near_device(*near[0])).wait_send()
        bytes_of(arrived.at[l], ssend.at[l], srecv.at[l, 0], far_device(far[0])).wait_send()

    def lower_copies(target):
        found = []
        for l in range(target):
            p = pair_of(levels, l, target)
            for kb in range(1, pair):
                found.append((p, pltpu.make_async_remote_copy(
                    src_ref=lower.at[p, :, (side + kb) % pair], dst_ref=held.at[p, kb - 1],
                    send_sem=lsend.at[p, kb - 1], recv_sem=lrecv.at[p, kb - 1],
                    device_id=near_device(0, kb), device_id_type=MESH,
                )))
        return found

    def source_copies():
        return [
            pltpu.make_async_remote_copy(
                src_ref=sources, dst_ref=far_sources.at[kb - 1],
                send_sem=csend.at[kb - 1], recv_sem=crecv.at[kb - 1],
                device_id=near_device(0, kb), device_id_type=MESH,
            )
            for kb in range(1, pair)
        ]

    lane = lax.broadcasted_iota(jnp.int32, (bs, 2 * bs), 1)
    first = lane < bs

    def spread(p, index_of, block_of, from_side):
        def one(g, carry):
            s0 = index_of(0, g * pair + side)
            s1 = index_of(1, g * pair + side)
            block = block_of(g)
            in_place = jnp.where(first, s0, s1)
            across = jnp.where(first, s1, s0)
            swapped = jnp.concatenate([block[:, bs:], block[:, :bs]], axis=1)
            for two in range(rows // 2):
                even, odd = 2 * two, 2 * two + 1
                wanted = jnp.where(first, even, odd)
                straight = jnp.where(in_place == wanted, 1.0, 0.0).astype(BF16)
                crossed = jnp.where(across == wanted, 1.0, 0.0).astype(BF16)
                wide[p, from_side, g, :, 2 * two * bs:(2 * two + 2) * bs] = (
                    block * straight + swapped * crossed
                )
            return carry

        if groups <= 4:
            for g in range(groups):
                one(g, 0)
        else:
            lax.fori_loop(0, groups, one, 0)

    def spread_own(target):
        for l in range(target):
            p = pair_of(levels, l, target)
            spread(p, lambda e, q, p=p: own_s[p, e, q], lambda g, p=p: mine[p, g], side)

    def spread_far(target):
        for p, copy in lower_copies(target):
            copy.wait_recv()
        for l in range(target):
            p = pair_of(levels, l, target)
            for kb in range(1, pair):
                spread(
                    p, lambda e, q, p=p, kb=kb: far_s[kb - 1, p, e, q],
                    lambda g, p=p, kb=kb: held[p, kb - 1, g],
                    (side + pair - kb) % pair,
                )

    chunk = min(groups, 4)

    def product(l, target, h, begin):
        p = pair_of(levels, l, target)
        total = None
        for s in range(pair):
            left = wide[p, s, pl.ds(begin, chunk)].reshape(chunk * bs, rows * bs)
            right = gathered[l, h, s * rows:(s + 1) * rows].reshape(rows * bs, part)
            term = jnp.dot(left, right, preferred_element_type=F32)
            total = term if total is None else total + term
        return total.reshape(chunk, bs, part)

    def over_chunks(body):
        if groups == chunk:
            body(0)
        else:
            def step(i, carry):
                body(i * chunk)
                return carry
            lax.fori_loop(0, groups // chunk, step, 0)

    def earlier_terms(l, h):
        def body(begin):
            total = product(0, l + 1, h, begin)
            for m in range(1, l):
                total = total + product(m, l + 1, h, begin)
            summed[l % 2, h, pl.ds(begin, chunk)] = total
        if l > 0:
            over_chunks(body)

    def newest_term(l, h):
        def body(begin):
            total = product(l, l + 1, h, begin)
            if l > 0:
                total = total + summed[l % 2, h, pl.ds(begin, chunk)]
            summed[l % 2, h, pl.ds(begin, chunk)] = total
            outgoing[l, h, pl.ds(begin, chunk)] = total.astype(BF16)
        over_chunks(body)

    loads[0].wait()
    loads[1].wait()
    for l in range(levels):
        high = dinv[l].astype(BF16)
        low = (dinv[l] - high.astype(F32)).astype(BF16)
        split[l] = jnp.concatenate([high, high, low, low], axis=1)
    for h in range(parts):
        solve(0, h)
    loads[2].wait()
    loads[3].wait()
    spread_own(1)
    pl.semaphore_wait(barrier, len(near) + 1 + len(far))
    for copy in source_copies():
        copy.start()

    for copy in gather_copies(0, 0):
        copy.start()
    for p, copy in lower_copies(1):
        copy.start()
    for l in range(last):
        for h in range(parts):
            if l > 0:
                wait_scatter(l - 1, h)
                solve(l, h)
                for copy in gather_copies(l, h):
                    copy.start()
                if h == 0:
                    spread_far(l + 1)
                    for k in range(parts):
                        earlier_terms(l, k)
        for h in range(parts):
            wait_gather(l, h)
            for copy in twin_copies(l, h):
                copy.start()
            if l == 0:
                if h + 1 < parts:
                    for copy in gather_copies(0, h + 1):
                        copy.start()
                if h == 0:
                    for i, copy in enumerate(source_copies()):
                        copy.wait_recv()
                        back = pltpu.make_async_copy(far_sources.at[i], far_s.at[i], local_sem.at[5 + i])
                        back.start()
                        back.wait()
                    spread_far(1)
            wait_twin(l, h)
            newest_term(l, h)
            for copy in scatter_copies(l, h):
                copy.start()
        if l + 1 < last:
            for p, copy in lower_copies(l + 2):
                copy.start()
            if l == 0:
                loads[4].wait()
            spread_own(l + 2)
            for p, copy in lower_copies(l + 1):
                copy.wait_send()
            if l > 0:
                wait_sends(l - 1)
    for copy in source_copies():
        copy.wait_send()
    for p, copy in lower_copies(last):
        copy.wait_send()
    for l in range(max(last - 2, 0), last - 1):
        wait_sends(l)
    for h in range(parts):
        wait_scatter(last - 1, h)
        solve(last, h)
    wait_sends(last - 1)

def in_hbm(x):
    return pltpu.with_memory_space_constraint(x, pltpu.HBM)


def on_device(rows, columns, rhs, dinv, lower, sources):
    levels, _, _, bs, width = rhs.shape
    pairs = lower.shape[0]
    per = sources.shape[-1]
    pair = 2
    parts = 2
    groups = columns // pair
    part = width // parts
    last = levels - 1
    far = groups - 1
    dma = pltpu.SemaphoreType.DMA
    flops = 2 * pairs * groups * bs * pair * rows * bs * width
    result = pl.pallas_call(
        functools.partial(kernel, rows, groups, pair, parts),
        out_shape=jax.ShapeDtypeStruct((levels, bs, width), F32),
        in_specs=[pl.BlockSpec(memory_space=pltpu.HBM)] * 4,
        out_specs=pl.BlockSpec(memory_space=pltpu.VMEM),
        scratch_shapes=[
            pltpu.VMEM((levels, bs, width), BF16),
            pltpu.VMEM((levels, bs, bs), F32),
            pltpu.VMEM((levels, bs, 4 * bs), BF16),
            pltpu.VMEM((pairs, groups, bs, per * bs), BF16),
            pltpu.VMEM((pairs, pair, groups, bs, rows * bs), BF16),
            pltpu.VMEM((pairs, pair - 1, groups, bs, per * bs), BF16),
            pltpu.VMEM((last, parts, pair * rows, bs, part), BF16),
            pltpu.VMEM((last, parts, groups, bs, part), BF16),
            pltpu.VMEM((last, parts, far, bs, part), BF16),
            pltpu.VMEM((2, parts, groups, bs, part), F32),
            pltpu.VMEM((pair - 1, pairs, per, columns), jnp.int32),
            pltpu.SMEM((pairs, per, columns), jnp.int32),
            pltpu.SMEM((pair - 1, pairs, per, columns), jnp.int32),
            dma((last,)),
            dma((last, parts)),
            dma((last,)),
            dma((last, parts)),
            dma((pairs, pair - 1)),
            dma((pairs, pair - 1)),
            dma((pair - 1,)),
            dma((pair - 1,)),
            dma((4 + pair,)),
            dma((last, parts)),
        ],
        compiler_params=pltpu.CompilerParams(
            collective_id=0, has_side_effects=True, vmem_limit_bytes=48*1024*1024
        ),
        cost_estimate=pl.CostEstimate(
            flops=flops, bytes_accessed=2 * lower.size, transcendentals=0
        ),
    )(
        in_hbm(rhs.reshape(levels, bs, width)),
        in_hbm(dinv.reshape(levels, bs, bs)),
        in_hbm(lower.reshape(pairs, groups, pair, bs, per * bs)),
        in_hbm(jnp.swapaxes(sources.reshape(pairs, columns, per), 1, 2)),
    )
    return result.reshape(levels, 1, 1, bs, width)


def solution(mesh):
    in_specs = (
        P(None, "row", "col", None, None),
        P(None, "row", "col", None, None),
        P(None, "row", "col", None, None, None),
        P(None, "row", "col", None, None),
    )
    out_specs = P(None, "row", "col", None, None)
    return jax.shard_map(
        functools.partial(on_device, mesh.shape["row"], mesh.shape["col"]),
        mesh=mesh, in_specs=in_specs, out_specs=out_specs, check_vma=False,
    )
```

```python
import functools

import jax
import jax.numpy as jnp
from jax import lax
from jax.experimental import pallas as pl
from jax.experimental.pallas import tpu as pltpu
from jax.sharding import PartitionSpec as P

MESH = pl.DeviceIdType.MESH
BF16 = jnp.bfloat16
F32 = jnp.float32


def pair_of(levels, solved, target):
    return sum(levels - 1 - l for l in range(solved)) + target - solved - 1


def kernel(
    rows, groups, pair, parts,
    rhs_hbm, dinv_hbm, lower, sources, out,
    rhs, dinv, split, mine, wide, held, gathered, outgoing, arrived, summed,
    far_sources, own_s, far_s,
    gsend, grecv, ssend, srecv, lsend, lrecv, csend, crecv, local_sem,
):
    levels, bs, width = rhs.shape
    part = width // parts
    last = levels - 1
    row = lax.axis_index("row")
    col = lax.axis_index("col")
    group = col // pair
    side = col % pair
    blocks = pair * rows

    loads = [
        pltpu.make_async_copy(rhs_hbm, rhs, local_sem.at[0]),
        pltpu.make_async_copy(dinv_hbm, dinv, local_sem.at[1]),
        pltpu.make_async_copy(sources, own_s, local_sem.at[2]),
        pltpu.make_async_copy(lower.at[0, :, side], mine.at[0], local_sem.at[3]),
        pltpu.make_async_copy(lower.at[1:, :, side], mine.at[1:], local_sem.at[4]),
    ]
    for load in loads:
        load.start()

    near = [(kr, kb) for kb in reversed(range(pair)) for kr in reversed(range(rows)) if (kr, kb) != (0, 0)]
    far = list(reversed(range(1, groups)))

    def near_device(kr, kb):
        return ((row + kr) % rows, group * pair + (side + kb) % pair)

    def far_device(ka):
        return (row, ((group + ka) % groups) * pair + side)

    barrier = pltpu.get_barrier_semaphore()
    for kr, kb in near:
        pl.semaphore_signal(barrier, inc=1, device_id=near_device(kr, kb), device_id_type=MESH)
    for ka in far:
        pl.semaphore_signal(barrier, inc=1, device_id=far_device(ka), device_id_type=MESH)

    def cols(h):
        return pl.ds(h * part, part)

    def solve(l, h):
        residual = rhs[l, :, cols(h)].astype(F32)
        if l > 0:
            acc = summed[h, group]
            for i in range(groups - 1):
                acc = acc + arrived[l - 1, h, i].astype(F32)
            residual = residual - acc
        high = residual.astype(BF16)
        low = (residual - high.astype(F32)).astype(BF16)
        solution = jnp.dot(
            split[l], jnp.concatenate([high, low, high, low], axis=0),
            preferred_element_type=F32,
        )
        out[l, :, cols(h)] = solution
        if l < last:
            gathered[l, h, side * rows + row] = solution.astype(BF16)

    def gather_copies(l, h):
        block = gathered.at[l, h, side * rows + row]
        return [
            pltpu.make_async_remote_copy(
                src_ref=block, dst_ref=block,
                send_sem=gsend.at[l], recv_sem=grecv.at[l, h],
                device_id=near_device(kr, kb), device_id_type=MESH,
            )
            for kr, kb in near
        ]

    def scatter_copies(l, h):
        return [
            pltpu.make_async_remote_copy(
                src_ref=outgoing.at[l, h, (group + ka) % groups], dst_ref=arrived.at[l, h, i],
                send_sem=ssend.at[l], recv_sem=srecv.at[l, h],
                device_id=far_device(ka), device_id_type=MESH,
            )
            for i, ka in enumerate(far)
        ]

    def bytes_of(ref, send_sem, recv_sem, device):
        return pltpu.make_async_remote_copy(
            src_ref=ref, dst_ref=ref, send_sem=send_sem, recv_sem=recv_sem,
            device_id=device, device_id_type=MESH,
        )

    def wait_gather(l, h):
        ref = gathered.at[l, h, pl.ds(0, blocks - 1)]
        bytes_of(ref, gsend.at[l], grecv.at[l, h], near_device(*near[0])).wait_recv()

    def wait_scatter(l, h):
        bytes_of(arrived.at[l, h], ssend.at[l], srecv.at[l, h], far_device(far[0])).wait_recv()

    def wait_sends(l):
        ref = gathered.at[l, :, pl.ds(0, blocks - 1)]
        bytes_of(ref, gsend.at[l], grecv.at[l, 0], near_device(*near[0])).wait_send()
        bytes_of(arrived.at[l], ssend.at[l], srecv.at[l, 0], far_device(far[0])).wait_send()

    def lower_copies(target):
        found = []
        for l in range(target):
            p = pair_of(levels, l, target)
            for kb in range(1, pair):
                found.append((p, pltpu.make_async_remote_copy(
                    src_ref=lower.at[p, :, (side + kb) % pair], dst_ref=held.at[p, kb - 1],
                    send_sem=lsend.at[p, kb - 1], recv_sem=lrecv.at[p, kb - 1],
                    device_id=near_device(0, kb), device_id_type=MESH,
                )))
        return found

    def source_copies():
        return [
            pltpu.make_async_remote_copy(
                src_ref=sources, dst_ref=far_sources.at[kb - 1],
                send_sem=csend.at[kb - 1], recv_sem=crecv.at[kb - 1],
                device_id=near_device(0, kb), device_id_type=MESH,
            )
            for kb in range(1, pair)
        ]

    lane = lax.broadcasted_iota(jnp.int32, (bs, 2 * bs), 1)
    first = lane < bs

    def spread(p, index_of, block_of, from_side):
        def one(g, carry):
            s0 = index_of(0, g * pair + side)
            s1 = index_of(1, g * pair + side)
            block = block_of(g)
            in_place = jnp.where(first, s0, s1)
            across = jnp.where(first, s1, s0)
            swapped = jnp.concatenate([block[:, bs:], block[:, :bs]], axis=1)
            for two in range(rows // 2):
                even, odd = 2 * two, 2 * two + 1
                wanted = jnp.where(first, even, odd)
                straight = jnp.where(in_place == wanted, 1.0, 0.0).astype(BF16)
                crossed = jnp.where(across == wanted, 1.0, 0.0).astype(BF16)
                wide[p, from_side, g, :, 2 * two * bs:(2 * two + 2) * bs] = (
                    block * straight + swapped * crossed
                )
            return carry

        if groups <= 4:
            for g in range(groups):
                one(g, 0)
        else:
            lax.fori_loop(0, groups, one, 0)

    def spread_own(target):
        for l in range(target):
            p = pair_of(levels, l, target)
            spread(p, lambda e, q, p=p: own_s[p, e, q], lambda g, p=p: mine[p, g], side)

    def spread_far(target):
        for p, copy in lower_copies(target):
            copy.wait_recv()
        for l in range(target):
            p = pair_of(levels, l, target)
            for kb in range(1, pair):
                spread(
                    p, lambda e, q, p=p, kb=kb: far_s[kb - 1, p, e, q],
                    lambda g, p=p, kb=kb: held[p, kb - 1, g],
                    (side + pair - kb) % pair,
                )

    chunk = min(groups, 4)

    def product(l, target, h, begin):
        p = pair_of(levels, l, target)
        total = None
        for s in range(pair):
            left = wide[p, s, pl.ds(begin, chunk)].reshape(chunk * bs, rows * bs)
            right = gathered[l, h, s * rows:(s + 1) * rows].reshape(rows * bs, part)
            term = jnp.dot(left, right, preferred_element_type=F32)
            total = term if total is None else total + term
        return total.reshape(chunk, bs, part)

    def over_chunks(body):
        if groups == chunk:
            body(0)
        else:
            def step(i, carry):
                body(i * chunk)
                return carry
            lax.fori_loop(0, groups // chunk, step, 0)

    def earlier_terms(l, h):
        def body(begin):
            total = product(0, l + 1, h, begin)
            for m in range(1, l):
                total = total + product(m, l + 1, h, begin)
            summed[h, pl.ds(begin, chunk)] = total
        if l > 0:
            over_chunks(body)

    def newest_term(l, h):
        def body(begin):
            total = product(l, l + 1, h, begin)
            if l > 0:
                total = total + summed[h, pl.ds(begin, chunk)]
            summed[h, pl.ds(begin, chunk)] = total
            outgoing[l, h, pl.ds(begin, chunk)] = total.astype(BF16)
        over_chunks(body)

    loads[0].wait()
    loads[1].wait()
    for l in range(levels):
        high = dinv[l].astype(BF16)
        low = (dinv[l] - high.astype(F32)).astype(BF16)
        split[l] = jnp.concatenate([high, high, low, low], axis=1)
    for h in range(parts):
        solve(0, h)
    loads[2].wait()
    loads[3].wait()
    spread_own(1)
    pl.semaphore_wait(barrier, len(near) + len(far))
    for copy in source_copies():
        copy.start()

    for l in range(last):
        for h in range(parts):
            if l > 0:
                wait_scatter(l - 1, h)
                solve(l, h)
            for copy in gather_copies(l, h):
                copy.start()
            if l == 0 and h == 0:
                for p, copy in lower_copies(1):
                    copy.start()
        if l == 0:
            for i, copy in enumerate(source_copies()):
                copy.wait_recv()
                back = pltpu.make_async_copy(far_sources.at[i], far_s.at[i], local_sem.at[5 + i])
                back.start()
                back.wait()
        spread_far(l + 1)
        for h in range(parts):
            earlier_terms(l, h)
        for h in range(parts):
            wait_gather(l, h)
            newest_term(l, h)
            for copy in scatter_copies(l, h):
                copy.start()
        if l + 1 < last:
            for p, copy in lower_copies(l + 2):
                copy.start()
            if l == 0:
                loads[4].wait()
            spread_own(l + 2)
            for p, copy in lower_copies(l + 1):
                copy.wait_send()
            if l > 0:
                wait_sends(l - 1)
    for copy in source_copies():
        copy.wait_send()
    for p, copy in lower_copies(last):
        copy.wait_send()
    for l in range(max(last - 2, 0), last - 1):
        wait_sends(l)
    for h in range(parts):
        wait_scatter(last - 1, h)
        solve(last, h)
    wait_sends(last - 1)

def in_hbm(x):
    return pltpu.with_memory_space_constraint(x, pltpu.HBM)


def on_device(rows, columns, rhs, dinv, lower, sources):
    levels, _, _, bs, width = rhs.shape
    pairs = lower.shape[0]
    per = sources.shape[-1]
    pair = 2
    parts = 2
    groups = columns // pair
    part = width // parts
    last = levels - 1
    far = groups - 1
    dma = pltpu.SemaphoreType.DMA
    flops = 2 * pairs * groups * bs * pair * rows * bs * width
    result = pl.pallas_call(
        functools.partial(kernel, rows, groups, pair, parts),
        out_shape=jax.ShapeDtypeStruct((levels, bs, width), F32),
        in_specs=[pl.BlockSpec(memory_space=pltpu.HBM)] * 4,
        out_specs=pl.BlockSpec(memory_space=pltpu.VMEM),
        scratch_shapes=[
            pltpu.VMEM((levels, bs, width), BF16),
            pltpu.VMEM((levels, bs, bs), F32),
            pltpu.VMEM((levels, bs, 4 * bs), BF16),
            pltpu.VMEM((pairs, groups, bs, per * bs), BF16),
            pltpu.VMEM((pairs, pair, groups, bs, rows * bs), BF16),
            pltpu.VMEM((pairs, pair - 1, groups, bs, per * bs), BF16),
            pltpu.VMEM((last, parts, pair * rows, bs, part), BF16),
            pltpu.VMEM((last, parts, groups, bs, part), BF16),
            pltpu.VMEM((last, parts, far, bs, part), BF16),
            pltpu.VMEM((parts, groups, bs, part), F32),
            pltpu.VMEM((pair - 1, pairs, per, columns), jnp.int32),
            pltpu.SMEM((pairs, per, columns), jnp.int32),
            pltpu.SMEM((pair - 1, pairs, per, columns), jnp.int32),
            dma((last,)),
            dma((last, parts)),
            dma((last,)),
            dma((last, parts)),
            dma((pairs, pair - 1)),
            dma((pairs, pair - 1)),
            dma((pair - 1,)),
            dma((pair - 1,)),
            dma((4 + pair,)),
        ],
        compiler_params=pltpu.CompilerParams(
            collective_id=0, has_side_effects=True, vmem_limit_bytes=48 * 1024 * 1024
        ),
        cost_estimate=pl.CostEstimate(
            flops=flops, bytes_accessed=2 * lower.size, transcendentals=0
        ),
    )(
        in_hbm(rhs.reshape(levels, bs, width)),
        in_hbm(dinv.reshape(levels, bs, bs)),
        in_hbm(lower.reshape(pairs, groups, pair, bs, per * bs)),
        in_hbm(jnp.swapaxes(sources.reshape(pairs, columns, per), 1, 2)),
    )
    return result.reshape(levels, 1, 1, bs, width)


def solution(mesh):
    in_specs = (
        P(None, "row", "col", None, None),
        P(None, "row", "col", None, None),
        P(None, "row", "col", None, None, None),
        P(None, "row", "col", None, None),
    )
    out_specs = P(None, "row", "col", None, None)
    return jax.shard_map(
        functools.partial(on_device, mesh.shape["row"], mesh.shape["col"]),
        mesh=mesh, in_specs=in_specs, out_specs=out_specs, check_vma=False,
    )
```

```python
import functools

import jax
import jax.numpy as jnp
from jax import lax
from jax.experimental import pallas as pl
from jax.experimental.pallas import tpu as pltpu
from jax.sharding import PartitionSpec as P

MESH = pl.DeviceIdType.MESH
BF16 = jnp.bfloat16
F32 = jnp.float32


def pair_of(levels, solved, target):
    return sum(levels - 1 - l for l in range(solved)) + target - solved - 1


def kernel(
    rows, groups, pair, parts,
    rhs_hbm, dinv_hbm, lower, sources, out,
    rhs, dinv, split, mine, wide, held, gathered, outgoing, arrived, summed,
    far_sources, own_s, far_s,
    gsend, grecv, ssend, srecv, lsend, lrecv, csend, crecv, local_sem,
):
    levels, bs, width = rhs.shape
    part = width // parts
    last = levels - 1
    row = lax.axis_index("row")
    col = lax.axis_index("col")
    group = col // pair
    side = col % pair
    blocks = pair * rows

    loads = [
        pltpu.make_async_copy(rhs_hbm, rhs, local_sem.at[0]),
        pltpu.make_async_copy(dinv_hbm, dinv, local_sem.at[1]),
        pltpu.make_async_copy(sources, own_s, local_sem.at[2]),
        pltpu.make_async_copy(lower.at[0, :, side], mine.at[0], local_sem.at[3]),
        pltpu.make_async_copy(lower.at[1:, :, side], mine.at[1:], local_sem.at[4]),
    ]
    for load in loads:
        load.start()

    near = [(kr, kb) for kb in reversed(range(pair)) for kr in reversed(range(rows)) if (kr, kb) != (0, 0)]
    far = list(reversed(range(1, groups)))

    def near_device(kr, kb):
        return ((row + kr) % rows, group * pair + (side + kb) % pair)

    def far_device(ka):
        return (row, ((group + ka) % groups) * pair + side)

    barrier = pltpu.get_barrier_semaphore()
    for kr, kb in near:
        pl.semaphore_signal(barrier, inc=1, device_id=near_device(kr, kb), device_id_type=MESH)
    for ka in far:
        pl.semaphore_signal(barrier, inc=1, device_id=far_device(ka), device_id_type=MESH)

    def cols(h):
        return pl.ds(h * part, part)

    def solve(l, h):
        residual = rhs[l, :, cols(h)].astype(F32)
        if l > 0:
            acc = summed[h, group]
            for i in range(groups - 1):
                acc = acc + arrived[l - 1, h, i].astype(F32)
            residual = residual - acc
        high = residual.astype(BF16)
        low = (residual - high.astype(F32)).astype(BF16)
        solution = jnp.dot(
            split[l], jnp.concatenate([high, low, high, low], axis=0),
            preferred_element_type=F32,
        )
        out[l, :, cols(h)] = solution
        if l < last:
            gathered[l, h, side * rows + row] = solution.astype(BF16)

    def gather_copies(l, h):
        block = gathered.at[l, h, side * rows + row]
        return [
            pltpu.make_async_remote_copy(
                src_ref=block, dst_ref=block,
                send_sem=gsend.at[l], recv_sem=grecv.at[l, h],
                device_id=near_device(kr, kb), device_id_type=MESH,
            )
            for kr, kb in near
        ]

    def scatter_copies(l, h):
        return [
            pltpu.make_async_remote_copy(
                src_ref=outgoing.at[l, h, (group + ka) % groups], dst_ref=arrived.at[l, h, i],
                send_sem=ssend.at[l], recv_sem=srecv.at[l, h],
                device_id=far_device(ka), device_id_type=MESH,
            )
            for i, ka in enumerate(far)
        ]

    def bytes_of(ref, send_sem, recv_sem, device):
        return pltpu.make_async_remote_copy(
            src_ref=ref, dst_ref=ref, send_sem=send_sem, recv_sem=recv_sem,
            device_id=device, device_id_type=MESH,
        )

    def wait_gather(l, h):
        ref = gathered.at[l, h, pl.ds(0, blocks - 1)]
        bytes_of(ref, gsend.at[l], grecv.at[l, h], near_device(*near[0])).wait_recv()

    def wait_scatter(l, h):
        bytes_of(arrived.at[l, h], ssend.at[l], srecv.at[l, h], far_device(far[0])).wait_recv()

    def wait_sends(l):
        ref = gathered.at[l, :, pl.ds(0, blocks - 1)]
        bytes_of(ref, gsend.at[l], grecv.at[l, 0], near_device(*near[0])).wait_send()
        bytes_of(arrived.at[l], ssend.at[l], srecv.at[l, 0], far_device(far[0])).wait_send()

    def lower_copies(target):
        found = []
        for l in range(target):
            p = pair_of(levels, l, target)
            for kb in range(1, pair):
                found.append((p, pltpu.make_async_remote_copy(
                    src_ref=lower.at[p, :, (side + kb) % pair], dst_ref=held.at[p, kb - 1],
                    send_sem=lsend.at[p, kb - 1], recv_sem=lrecv.at[p, kb - 1],
                    device_id=near_device(0, kb), device_id_type=MESH,
                )))
        return found

    def source_copies():
        return [
            pltpu.make_async_remote_copy(
                src_ref=sources, dst_ref=far_sources.at[kb - 1],
                send_sem=csend.at[kb - 1], recv_sem=crecv.at[kb - 1],
                device_id=near_device(0, kb), device_id_type=MESH,
            )
            for kb in range(1, pair)
        ]

    lane = lax.broadcasted_iota(jnp.int32, (bs, 2 * bs), 1)
    first = lane < bs

    def spread(p, index_of, block_of, from_side):
        def one(g, carry):
            s0 = index_of(0, g * pair + side)
            s1 = index_of(1, g * pair + side)
            block = block_of(g)
            in_place = jnp.where(first, s0, s1)
            across = jnp.where(first, s1, s0)
            swapped = jnp.concatenate([block[:, bs:], block[:, :bs]], axis=1)
            for two in range(rows // 2):
                even, odd = 2 * two, 2 * two + 1
                wanted = jnp.where(first, even, odd)
                straight = jnp.where(in_place == wanted, 1.0, 0.0).astype(BF16)
                crossed = jnp.where(across == wanted, 1.0, 0.0).astype(BF16)
                wide[p, from_side, g, :, 2 * two * bs:(2 * two + 2) * bs] = (
                    block * straight + swapped * crossed
                )
            return carry

        if groups <= 4:
            for g in range(groups):
                one(g, 0)
        else:
            lax.fori_loop(0, groups, one, 0)

    def spread_own(target):
        for l in range(target):
            p = pair_of(levels, l, target)
            spread(p, lambda e, q, p=p: own_s[p, e, q], lambda g, p=p: mine[p, g], side)

    def spread_far(target):
        for p, copy in lower_copies(target):
            copy.wait_recv()
        for l in range(target):
            p = pair_of(levels, l, target)
            for kb in range(1, pair):
                spread(
                    p, lambda e, q, p=p, kb=kb: far_s[kb - 1, p, e, q],
                    lambda g, p=p, kb=kb: held[p, kb - 1, g],
                    (side + pair - kb) % pair,
                )

    chunk = min(groups, 4)

    def product(l, target, h, begin):
        p = pair_of(levels, l, target)
        total = None
        for s in range(pair):
            left = wide[p, s, pl.ds(begin, chunk)].reshape(chunk * bs, rows * bs)
            right = gathered[l, h, s * rows:(s + 1) * rows].reshape(rows * bs, part)
            term = jnp.dot(left, right, preferred_element_type=F32)
            total = term if total is None else total + term
        return total.reshape(chunk, bs, part)

    def over_chunks(body):
        if groups == chunk:
            body(0)
        else:
            def step(i, carry):
                body(i * chunk)
                return carry
            lax.fori_loop(0, groups // chunk, step, 0)

    def earlier_terms(l, h):
        def body(begin):
            total = product(0, l + 1, h, begin)
            for m in range(1, l):
                total = total + product(m, l + 1, h, begin)
            summed[h, pl.ds(begin, chunk)] = total
        if l > 0:
            over_chunks(body)

    def newest_term(l, h):
        def body(begin):
            total = product(l, l + 1, h, begin)
            if l > 0:
                total = total + summed[h, pl.ds(begin, chunk)]
            summed[h, pl.ds(begin, chunk)] = total
            outgoing[l, h, pl.ds(begin, chunk)] = total.astype(BF16)
        over_chunks(body)

    loads[0].wait()
    loads[1].wait()
    for l in range(levels):
        high = dinv[l].astype(BF16)
        low = (dinv[l] - high.astype(F32)).astype(BF16)
        split[l] = jnp.concatenate([high, high, low, low], axis=1)
    for h in range(parts):
        solve(0, h)
    loads[2].wait()
    loads[3].wait()
    spread_own(1)
    pl.semaphore_wait(barrier, len(near) + len(far))
    for copy in source_copies():
        copy.start()

    for l in range(last):
        for h in range(parts):
            if l > 0:
                wait_scatter(l - 1, h)
                solve(l, h)
            for copy in gather_copies(l, h):
                copy.start()
            if l == 0 and h == 0:
                for p, copy in lower_copies(1):
                    copy.start()
        if l == 0:
            for i, copy in enumerate(source_copies()):
                copy.wait_recv()
                back = pltpu.make_async_copy(far_sources.at[i], far_s.at[i], local_sem.at[5 + i])
                back.start()
                back.wait()
        spread_far(l + 1)
        for h in range(parts):
            earlier_terms(l, h)
        for h in range(parts):
            wait_gather(l, h)
            newest_term(l, h)
            for copy in scatter_copies(l, h):
                copy.start()
        if l + 1 < last:
            for p, copy in lower_copies(l + 2):
                copy.start()
            if l == 0:
                loads[4].wait()
            spread_own(l + 2)
            for p, copy in lower_copies(l + 1):
                copy.wait_send()
            if l > 0:
                wait_sends(l - 1)
    for copy in source_copies():
        copy.wait_send()
    for p, copy in lower_copies(last):
        copy.wait_send()
    for l in range(max(last - 2, 0), last - 1):
        wait_sends(l)
    for h in range(parts):
        wait_scatter(last - 1, h)
        solve(last, h)
    wait_sends(last - 1)

def in_hbm(x):
    return pltpu.with_memory_space_constraint(x, pltpu.HBM)


def on_device(rows, columns, rhs, dinv, lower, sources):
    levels, _, _, bs, width = rhs.shape
    pairs = lower.shape[0]
    per = sources.shape[-1]
    pair = 2
    parts = 1
    groups = columns // pair
    part = width // parts
    last = levels - 1
    far = groups - 1
    dma = pltpu.SemaphoreType.DMA
    flops = 2 * pairs * groups * bs * pair * rows * bs * width
    result = pl.pallas_call(
        functools.partial(kernel, rows, groups, pair, parts),
        out_shape=jax.ShapeDtypeStruct((levels, bs, width), F32),
        in_specs=[pl.BlockSpec(memory_space=pltpu.HBM)] * 4,
        out_specs=pl.BlockSpec(memory_space=pltpu.VMEM),
        scratch_shapes=[
            pltpu.VMEM((levels, bs, width), BF16),
            pltpu.VMEM((levels, bs, bs), F32),
            pltpu.VMEM((levels, bs, 4 * bs), BF16),
            pltpu.VMEM((pairs, groups, bs, per * bs), BF16),
            pltpu.VMEM((pairs, pair, groups, bs, rows * bs), BF16),
            pltpu.VMEM((pairs, pair - 1, groups, bs, per * bs), BF16),
            pltpu.VMEM((last, parts, pair * rows, bs, part), BF16),
            pltpu.VMEM((last, parts, groups, bs, part), BF16),
            pltpu.VMEM((last, parts, far, bs, part), BF16),
            pltpu.VMEM((parts, groups, bs, part), F32),
            pltpu.VMEM((pair - 1, pairs, per, columns), jnp.int32),
            pltpu.SMEM((pairs, per, columns), jnp.int32),
            pltpu.SMEM((pair - 1, pairs, per, columns), jnp.int32),
            dma((last,)),
            dma((last, parts)),
            dma((last,)),
            dma((last, parts)),
            dma((pairs, pair - 1)),
            dma((pairs, pair - 1)),
            dma((pair - 1,)),
            dma((pair - 1,)),
            dma((4 + pair,)),
        ],
        compiler_params=pltpu.CompilerParams(
            collective_id=0, has_side_effects=True, vmem_limit_bytes=48 * 1024 * 1024
        ),
        cost_estimate=pl.CostEstimate(
            flops=flops, bytes_accessed=2 * lower.size, transcendentals=0
        ),
    )(
        in_hbm(rhs.reshape(levels, bs, width)),
        in_hbm(dinv.reshape(levels, bs, bs)),
        in_hbm(lower.reshape(pairs, groups, pair, bs, per * bs)),
        in_hbm(jnp.swapaxes(sources.reshape(pairs, columns, per), 1, 2)),
    )
    return result.reshape(levels, 1, 1, bs, width)


def solution(mesh):
    in_specs = (
        P(None, "row", "col", None, None),
        P(None, "row", "col", None, None),
        P(None, "row", "col", None, None, None),
        P(None, "row", "col", None, None),
    )
    out_specs = P(None, "row", "col", None, None)
    return jax.shard_map(
        functools.partial(on_device, mesh.shape["row"], mesh.shape["col"]),
        mesh=mesh, in_specs=in_specs, out_specs=out_specs, check_vma=False,
    )
```
